32 devices in a mesh: orb: 8 (over y, x, core), probe: 4 (over z).
Axes of the slice: x: 2, y: 2, z: 4, core: 2. Of those that a mesh axis runs over, the one named last changes fastest.
Arguments:
- tiles: bfloat16 [32, 9, 256, 256], P('orb', None, 'probe'), may hold values from -0.0625 to 0.0625
- pattern: int32 [32, 9], P('orb'), may hold values from 0 to 1, as said below
- signs: int32 [8192, 512], P('orb', 'probe'), may hold values from 0 to 1
- previous: bfloat16 [8192, 512], P('orb', 'probe'), may hold values from -6 to 6
- current: bfloat16 [8192, 512], P('orb', 'probe'), may hold values from -6 to 6
Outputs:
- older: bfloat16 [8192, 512], P('orb', 'probe')
- newest: bfloat16 [8192, 512], P('orb', 'probe')
- moments: float32 [4, 512], P(None, 'probe')
The draws below stay inside these ranges and needn't reach their ends.
Inputs may be any that keep to these rules, and one draw needn't show every extreme that they name: pattern[I, 4] is 1 for every row block; each row block has 4 to 9 ones; the 4 row blocks of one index of orb hold at most 28 ones together, and some index of orb holds exactly 28.
All inputs are finite; a program needn't handle non-finite values.
Results may differ from the reference program's by a relative error of at most 0.0053.
Values may be sent and summed in bfloat16 or wider, within the bound.
A program may use at most 64 MiB of HBM per device.

```python
import math
import jax
import jax.numpy as jnp
from jax import lax

BS = 256
REACH = 4
OFFS = 9
RB = 4
STEPS = 4
NB = 32
ORB = 8192
PROBES = 512


def draw_pattern(key, part):
    devices = NB // RB
    key_a, key_b, key_c = jax.random.split(jax.random.fold_in(key, 17), 3)
    extra = jax.random.randint(key_a, (devices, RB), 0, 6)
    total = jnp.sum(extra, axis=1, keepdims=True)
    limit = 3 * RB
    extra = jnp.where(total > limit, extra * limit // jnp.maximum(total, 1), extra)
    chosen = jax.random.randint(key_b, (), 0, devices)
    rest = 3 * RB - 5
    spread = (rest + jnp.arange(RB - 2)) // (RB - 2)
    forced = jnp.concatenate([jnp.array([5, 0], jnp.int32), spread.astype(jnp.int32)])
    extra = jnp.where(jnp.arange(devices)[:, None] == chosen, forced[None, :], extra.astype(jnp.int32))
    extra = extra.reshape(NB)
    scores = jax.random.randint(key_c, (NB, OFFS - 1), 0, 1 << 20) * OFFS + jnp.arange(OFFS - 1)
    ranks = jnp.argsort(jnp.argsort(scores, axis=1), axis=1)
    live = (ranks < (3 + extra)[:, None]).astype(jnp.int32)
    middle = jnp.ones((NB, 1), jnp.int32)
    return jnp.concatenate([live[:, :REACH], middle, live[:, REACH:]], axis=1)


def with_ends(values, stream_key, low, high):
    longest = values.shape.index(max(values.shape))
    spots = []
    for shift in (0, 1):
        where = [jax.random.randint(jax.random.fold_in(stream_key, axis), (), 0, length) for axis, length in enumerate(values.shape)]
        where[longest] = (where[longest] + shift) % values.shape[longest]
        spots.append(tuple(where))
    return values.at[spots[0]].set(low).at[spots[1]].set(high)


def block_levels(stream_key, extent, pieces, smallest, high):
    level = 1.0
    for axis_at, shards_of in pieces:
        steps = jax.random.uniform(jax.random.fold_in(jax.random.fold_in(stream_key, 6), axis_at), (shards_of,), jnp.float32, smallest / len(pieces), high / len(pieces))
        level = level * jnp.repeat(jnp.exp(steps), extent[axis_at] // shards_of).reshape((-1,) + (1,) * (len(extent) - 1 - axis_at))
    return level


def normal_values(key, extent, scale, reach, cuts=(), held_as=jnp.bfloat16):
    values = jax.random.normal(key, extent, jnp.float32) * scale
    if len(cuts) > 0:
        values = block_levels(key, extent, cuts, -0.22, 0.18) * values
    return jnp.clip(values, min=-reach, max=reach).astype(held_as)


def setup_inputs(seed: int = 0) -> dict:
    splits = jax.random.split(jax.random.key(seed), 6)
    tiles = normal_values(splits[0], (NB, OFFS, BS, BS), (4 * OFFS * BS) ** -0.5, 0.0625, ((0, 8), (2, 4)))
    pattern = draw_pattern(jax.random.fold_in(splits[5], 71), 0)
    signs = with_ends(jax.random.randint(splits[2], (ORB, PROBES), 0, 2), jax.random.fold_in(splits[2], 1), 0, 1).astype(jnp.int32)
    previous = normal_values(splits[3], (ORB, PROBES), 1.0, 6.0, ((0, 8), (1, 4)))
    current = normal_values(splits[4], (ORB, PROBES), 1.0, 6.0, ((0, 8), (1, 4)))
    return dict(tiles=tiles, pattern=pattern, signs=signs, previous=previous, current=current)


def apply_operator(tiles, pattern, vec):
    blocks = vec.reshape(NB, BS, PROBES)
    mask_f = pattern.astype(jnp.float32)
    total = jnp.zeros((NB, BS, PROBES), jnp.float32)
    for offset in range(OFFS):
        moved = jnp.roll(blocks, -(offset - REACH), axis=0)
        product = jnp.einsum('bij,bjp->bip', tiles[:, offset].astype(jnp.float32), moved.astype(jnp.float32))
        total = total + mask_f[:, offset][:, None, None] * product
    return total.reshape(NB * BS, PROBES)

def reference(tiles, pattern, signs, previous, current):
    sign_f = (2 * signs - 1).astype(jnp.float32)
    factor = 1.0 / math.sqrt(ORB)
    older, newest = (previous, current)
    gathered = []
    for step in range(STEPS):
        image = apply_operator(tiles, pattern, newest)
        nxt = (2.0 * image - older.astype(jnp.float32)).astype(jnp.bfloat16)
        gathered.append(lax.optimization_barrier(jnp.sum(sign_f * nxt.astype(jnp.float32), axis=0)) * factor)
        older, newest = (newest, nxt)
    return (older, newest, jnp.stack(gathered))
```

```python
import functools
import math

import jax
import jax.numpy as jnp
from jax import lax
from jax.experimental import pallas as pl
from jax.experimental.pallas import tpu as pltpu
from jax.sharding import PartitionSpec as P

STEPS = 4
LIVE_PER_ROW = 7
LEAST_PER_ROW = 4
MESH = pl.DeviceIdType.MESH


def chunk_bounds(row_blocks, offsets):
    slots = LIVE_PER_ROW * row_blocks
    return [
        min(offsets * (i + 1), slots - LEAST_PER_ROW * (row_blocks - 1 - i))
        for i in range(row_blocks)
    ]


def kernel(
    n_orb, n_probe, rb, offs, rows, bs, pc,
    pattern_ref, tiles_hbm, signs_hbm, previous_hbm, current_hbm,
    older_hbm, newest_hbm, moments_ref,
    tl, signs, prev, full, stage, dense, win, last, acc, mbuf, slot_of, nxt,
    in_sem, out_sem, g_send, g_recv, h_send, h_recv, m_send, m_recv,
):
    slots = LIVE_PER_ROW * rb
    span = rb * bs
    depth = offs * bs
    bounds = chunk_bounds(rb, offs)
    chunks = list(zip([0] + bounds[:-1], bounds))
    orb = lax.axis_index("orb")
    z = lax.axis_index("probe")
    up = lax.rem(orb + 1, n_orb)
    down = lax.rem(orb + n_orb - 1, n_orb)

    loads = [
        pltpu.make_async_copy(tiles_hbm, tl, in_sem.at[0]),
        pltpu.make_async_copy(current_hbm, win.at[0, pl.ds(span, span)], in_sem.at[1]),
        pltpu.make_async_copy(previous_hbm, prev, in_sem.at[2]),
        pltpu.make_async_copy(signs_hbm, signs, in_sem.at[3]),
    ]
    for load in loads:
        load.start()

    barrier = pltpu.get_barrier_semaphore()

    def greet(j, carry):
        pl.semaphore_signal(
            barrier, inc=1, device_id=(lax.rem(orb + j, n_orb), z), device_id_type=MESH
        )
        return carry

    lax.fori_loop(1, n_orb, greet, 0)

    @pl.when(z > 0)
    def _():
        pl.semaphore_signal(barrier, inc=1, device_id=(orb, z - 1), device_id_type=MESH)

    @pl.when(z < n_probe - 1)
    def _():
        pl.semaphore_signal(barrier, inc=1, device_id=(orb, z + 1), device_id_type=MESH)

    count = jnp.int32(0)
    for j in range(rb * offs):
        live = pattern_ref[j // offs, j % offs] == 1
        slot_of[j] = jnp.where(live, count, slots)
        count = count + live.astype(jnp.int32)
    following = jnp.int32(rb * offs - 1)
    nxt[rb * offs] = following
    for j in reversed(range(rb * offs)):
        live = pattern_ref[j // offs, j % offs] == 1
        following = jnp.where(live, j, following)
        nxt[j] = following
    stage[slots] = jnp.zeros((rows, bs), stage.dtype)

    loads[0].wait()
    at = nxt[0]
    for s in range(slots):
        full[z, s] = tl[at]
        at = nxt[at + 1]

    ends = (z > 0).astype(jnp.int32) + (z < n_probe - 1).astype(jnp.int32)
    pl.semaphore_wait(barrier, n_orb - 1 + ends)

    def tile_copy(side, d, c, q):
        lo, hi = chunks[c]
        piece = full.at[q, pl.ds(lo, hi - lo)]
        to = z + 1 if side == 0 else z - 1
        return pltpu.make_async_remote_copy(
            src_ref=piece, dst_ref=piece,
            send_sem=g_send.at[side, d - 1], recv_sem=g_recv.at[side, d - 1, c],
            device_id=(orb, to), device_id_type=MESH,
        )

    has_next = (z < n_probe - 1, z > 0)
    for c in range(rb):
        for side in range(2):
            @pl.when(has_next[side])
            def _():
                tile_copy(side, 1, c, z).start()

    def halo_copy(k, way, start, size):
        src = win.at[k, pl.ds(span + start, size)]
        dst = win.at[k, pl.ds((0 if way == 0 else 2 * span) + start, size)]
        return pltpu.make_async_remote_copy(
            src_ref=src, dst_ref=dst,
            send_sem=h_send.at[k, way], recv_sem=h_recv.at[k, way],
            device_id=(up if way == 0 else down, z), device_id_type=MESH,
        )

    loads[1].wait()
    for way in range(2):
        halo_copy(0, way, 0, span).start()
    loads[2].wait()

    def first_step(i, q):
        base = pl.multiple_of(q * rows, rows)
        total = jnp.dot(
            dense[i, pl.ds(base, rows), :],
            win[0, pl.ds(i * bs, depth), :],
            preferred_element_type=jnp.float32,
        )
        here = pl.multiple_of(i * bs + q * rows, rows)
        before = prev[pl.ds(here, rows), :].astype(jnp.float32)
        win[1, pl.ds(pl.multiple_of(span + here, rows), rows), :] = (
            2.0 * total - before
        ).astype(win.dtype)
        for way in range(2):
            halo_copy(1, way, here, rows).start()

    base_z = pl.multiple_of(z * rows, rows)
    for i in range(rb):
        for o in range(offs):
            mask = pattern_ref[i, o].astype(jnp.float32).astype(tl.dtype)
            dense[i, pl.ds(base_z, rows), o * bs:(o + 1) * bs] = tl[i * offs + o] * mask
    for way in range(2):
        halo_copy(0, way, 0, span).wait_recv()
    for i in range(rb):
        first_step(i, z)

    def hop(d, carry):
        for c in range(rb):
            lo, hi = chunks[c]
            for side in range(2):
                q = z - d if side == 0 else z + d
                valid = q >= 0 if side == 0 else q < n_probe

                @pl.when(valid)
                def _():
                    tile_copy(side, d, c, q).wait_recv()

                    @pl.when(has_next[side])
                    def _():
                        tile_copy(side, d + 1, c, q).start()

            for side in range(2):
                q = z - d if side == 0 else z + d
                valid = q >= 0 if side == 0 else q < n_probe

                @pl.when(valid)
                def _():
                    for s in range(lo, hi):
                        stage[s + side * (slots + 1)] = full[q, s]
                    base = pl.multiple_of(q * rows, rows)
                    for o in range(offs):
                        dense[c, pl.ds(base, rows), o * bs:(o + 1) * bs] = stage[
                            slot_of[c * offs + o] + side * (slots + 1)
                        ]
                    first_step(c, q)
        return carry

    stage[2 * slots + 1] = jnp.zeros((rows, bs), stage.dtype)
    lax.fori_loop(1, n_probe, hop, 0)
    loads[3].wait()

    def moment(value, start):
        sign = (2 * signs[pl.ds(start, bs), :] - 1).astype(jnp.float32)
        return jnp.sum(sign * value.astype(jnp.float32), axis=0, keepdims=True)

    def dot(i, first, blocks, k):
        return jnp.dot(
            dense[i, :, (first - i) * bs:(first - i + blocks) * bs],
            win[k, pl.ds(first * bs, blocks * bs), :],
            preferred_element_type=jnp.float32,
        )

    sums = []
    outs = []
    for k in range(2, STEPS + 1):
        for i in range(rb):
            acc[i] = dot(i, rb, rb, k - 1)
        total = jnp.zeros((1, pc), jnp.float32)
        for i in range(rb):
            total += moment(win[k - 1, pl.ds(span + i * bs, bs), :], i * bs)
        sums.append(total)
        for way in range(2):
            halo_copy(k - 1, way, 0, span).wait_recv()
        last_sum = jnp.zeros((1, pc), jnp.float32)
        for i in range(rb):
            image = acc[i] + dot(i, i, rb - i, k - 1) + dot(i, 2 * rb, i + 1, k - 1)
            before = win[k - 2, pl.ds(span + i * bs, bs), :].astype(jnp.float32)
            value = (2.0 * image - before).astype(win.dtype)
            if k < STEPS:
                win[k, pl.ds(span + i * bs, bs), :] = value
                for way in range(2):
                    halo_copy(k, way, i * bs, bs).start()
            else:
                last[pl.ds(i * bs, bs), :] = value
                last_sum += moment(value, i * bs)
        if k == STEPS - 1:
            outs.append(
                pltpu.make_async_copy(win.at[k, pl.ds(span, span)], older_hbm, out_sem.at[0])
            )
            outs[-1].start()
        if k == STEPS:
            sums.append(last_sum)
            outs.append(pltpu.make_async_copy(last, newest_hbm, out_sem.at[1]))
            outs[-1].start()

    mbuf[orb, 0:STEPS, :] = jnp.concatenate(sums, axis=0)

    def moment_copy(j):
        return pltpu.make_async_remote_copy(
            src_ref=mbuf.at[orb], dst_ref=mbuf.at[orb],
            send_sem=m_send, recv_sem=m_recv,
            device_id=(lax.rem(orb + j, n_orb), z), device_id_type=MESH,
        )

    def send_moment(j, carry):
        moment_copy(j).start()
        return carry

    lax.fori_loop(1, n_orb, send_moment, 0)

    for k in range(STEPS):
        for way in range(2):
            halo_copy(k, way, 0, span).wait_send()

    def sent(d, carry):
        for side in range(2):
            q = z + 1 - d if side == 0 else z - 1 + d
            valid = q >= 0 if side == 0 else q < n_probe

            @pl.when(jnp.logical_and(valid, has_next[side]))
            def _():
                pltpu.make_async_remote_copy(
                    src_ref=full.at[q], dst_ref=full.at[q],
                    send_sem=g_send.at[side, d - 1], recv_sem=g_recv.at[side, d - 1, 0],
                    device_id=(orb, z + 1 if side == 0 else z - 1), device_id_type=MESH,
                ).wait_send()
        return carry

    lax.fori_loop(1, n_probe, sent, 0)

    others = mbuf.at[pl.ds(0, n_orb - 1)]
    arrived = pltpu.make_async_remote_copy(
        src_ref=others, dst_ref=others, send_sem=m_send, recv_sem=m_recv,
        device_id=(up, z), device_id_type=MESH,
    )
    arrived.wait_recv()
    arrived.wait_send()
    result = mbuf[0]
    for j in range(1, n_orb):
        result = result + mbuf[j]
    moments_ref[...] = result[0:STEPS] * (1.0 / math.sqrt(n_orb * span))
    for out in outs:
        out.wait()


def body(tiles, pattern, signs, previous, current):
    n_orb, n_probe = lax.axis_size("orb"), lax.axis_size("probe")
    rb, offs, rows, bs = tiles.shape
    pc = previous.shape[1]
    slots = LIVE_PER_ROW * rb
    span = rb * bs
    bf16, f32 = jnp.bfloat16, jnp.float32
    anywhere = pl.BlockSpec(memory_space=pl.ANY)
    older, newest, moments = pl.pallas_call(
        functools.partial(kernel, n_orb, n_probe, rb, offs, rows, bs, pc),
        out_shape=(
            jax.ShapeDtypeStruct((span, pc), bf16),
            jax.ShapeDtypeStruct((span, pc), bf16),
            jax.ShapeDtypeStruct((STEPS, pc), f32),
        ),
        in_specs=[pl.BlockSpec(memory_space=pltpu.SMEM)] + [anywhere] * 4,
        out_specs=(anywhere, anywhere, pl.BlockSpec(memory_space=pltpu.VMEM)),
        scratch_shapes=[
            pltpu.VMEM((rb * offs, rows, bs), bf16),
            pltpu.VMEM((span, pc), jnp.int32),
            pltpu.VMEM((span, pc), bf16),
            pltpu.VMEM((n_probe, slots, rows, bs), bf16),
            pltpu.VMEM((2 * (slots + 1), rows, bs), bf16),
            pltpu.VMEM((rb, bs, offs * bs), bf16),
            pltpu.VMEM((STEPS, 3 * span, pc), bf16),
            pltpu.VMEM((span, pc), bf16),
            pltpu.VMEM((rb, bs, pc), f32),
            pltpu.VMEM((n_orb, 8, pc), f32),
            pltpu.SMEM((rb * offs,), jnp.int32),
            pltpu.SMEM((rb * offs + 1,), jnp.int32),
            pltpu.SemaphoreType.DMA((4,)),
            pltpu.SemaphoreType.DMA((2,)),
            pltpu.SemaphoreType.DMA((2, n_probe - 1)),
            pltpu.SemaphoreType.DMA((2, n_probe - 1, rb)),
            pltpu.SemaphoreType.DMA((STEPS, 2)),
            pltpu.SemaphoreType.DMA((STEPS, 2)),
            pltpu.SemaphoreType.DMA,
            pltpu.SemaphoreType.DMA,
        ],
        compiler_params=pltpu.CompilerParams(
            collective_id=0, has_side_effects=True, vmem_limit_bytes=40 * 2**20
        ),
    )(pattern, tiles.reshape(rb * offs, rows, bs), signs, previous, current)
    return older, newest, moments


def solution(mesh):
    placed = (
        P("orb", None, "probe", None),
        P("orb", None),
        P("orb", "probe"),
        P("orb", "probe"),
        P("orb", "probe"),
    )
    return jax.shard_map(
        body,
        mesh=mesh,
        in_specs=placed,
        out_specs=(P("orb", "probe"), P("orb", "probe"), P(None, "probe")),
        check_vma=False,
    )
```

```python
import functools
import math

import jax
import jax.numpy as jnp
from jax import lax
from jax.experimental import pallas as pl
from jax.experimental.pallas import tpu as pltpu
from jax.sharding import PartitionSpec as P

STEPS = 4
LIVE_PER_ROW = 7
LEAST_PER_ROW = 4
MESH = pl.DeviceIdType.MESH


def chunk_bounds(row_blocks, offsets):
    slots = LIVE_PER_ROW * row_blocks
    return [
        min(offsets * (i + 1), slots - LEAST_PER_ROW * (row_blocks - 1 - i))
        for i in range(row_blocks)
    ]


def kernel(
    n_orb, n_probe, rb, offs, rows, bs, pc,
    pattern_hbm, tiles_hbm, signs_hbm, previous_hbm, current_hbm,
    older_hbm, newest_hbm, moments_ref,
    tl, signs, prev, full, stage, dense, win, last, acc, mbuf, hwin, hprev, hout, pattern_ref, slot_of, nxt,
    in_sem, out_sem, g_send, g_recv, h_send, h_recv, m_send, m_recv,
    e_send, e_recv, eh_send, eh_recv, r_send, r_recv,
):
    slots = LIVE_PER_ROW * rb
    span = rb * bs
    depth = offs * bs
    bounds = chunk_bounds(rb, offs)
    chunks = list(zip([0] + bounds[:-1], bounds))
    orb = lax.axis_index("orb")
    z = lax.axis_index("probe")
    up = lax.rem(orb + 1, n_orb)
    down = lax.rem(orb + n_orb - 1, n_orb)

    loads = [
        pltpu.make_async_copy(tiles_hbm, tl, in_sem.at[0]),
        pltpu.make_async_copy(current_hbm, win.at[0, pl.ds(span, span)], in_sem.at[1]),
        pltpu.make_async_copy(previous_hbm, prev, in_sem.at[2]),
        pltpu.make_async_copy(signs_hbm, signs, in_sem.at[3]),
        pltpu.make_async_copy(pattern_hbm, pattern_ref, in_sem.at[4]),
    ]
    for load in loads:
        load.start()

    barrier = pltpu.get_barrier_semaphore()

    def greet(j, carry):
        pl.semaphore_signal(
            barrier, inc=1, device_id=(lax.rem(orb + j, n_orb), z), device_id_type=MESH
        )
        return carry

    lax.fori_loop(1, n_orb, greet, 0)

    @pl.when(z > 0)
    def _():
        pl.semaphore_signal(barrier, inc=1, device_id=(orb, z - 1), device_id_type=MESH)

    @pl.when(z < n_probe - 1)
    def _():
        pl.semaphore_signal(barrier, inc=1, device_id=(orb, z + 1), device_id_type=MESH)

    loads[4].wait()
    count = jnp.int32(0)
    for j in range(rb * offs):
        live = pattern_ref[j // offs, j % offs] == 1
        slot_of[j] = jnp.where(live, count, slots)
        count = count + live.astype(jnp.int32)
    following = jnp.int32(rb * offs - 1)
    nxt[rb * offs] = following
    for j in reversed(range(rb * offs)):
        live = pattern_ref[j // offs, j % offs] == 1
        following = jnp.where(live, j, following)
        nxt[j] = following
    stage[slots] = jnp.zeros((rows, bs), stage.dtype)

    loads[0].wait()
    at = nxt[0]
    for s in range(slots):
        full[z, s] = tl[at]
        at = nxt[at + 1]

    ends = (z > 0).astype(jnp.int32) + (z < n_probe - 1).astype(jnp.int32)
    pl.semaphore_wait(barrier, n_orb - 1 + ends)

    def tile_copy(side, d, c, q):
        lo, hi = chunks[c]
        piece = full.at[q, pl.ds(lo, hi - lo)]
        to = z + 1 if side == 0 else z - 1
        return pltpu.make_async_remote_copy(
            src_ref=piece, dst_ref=piece,
            send_sem=g_send.at[side, d - 1], recv_sem=g_recv.at[side, d - 1, c],
            device_id=(orb, to), device_id_type=MESH,
        )

    has_next = (z < n_probe - 1, z > 0)
    for c in range(rb):
        for side in range(2):
            @pl.when(has_next[side])
            def _():
                tile_copy(side, 1, c, z).start()

    low = z < n_probe // 2
    is_end = jnp.logical_or(z == 0, z == n_probe - 1)
    helps = jnp.logical_or(z == 1, z == n_probe - 2)
    partner = jnp.where(
        is_end, jnp.where(low, 1, n_probe - 2), jnp.where(low, 0, n_probe - 1)
    )
    far = jnp.where(low, n_probe - 1, 0)

    def lend_copy(src, dst, which):
        return pltpu.make_async_remote_copy(
            src_ref=src, dst_ref=dst,
            send_sem=e_send.at[which], recv_sem=e_recv.at[which],
            device_id=(orb, partner), device_id_type=MESH,
        )

    def lent_vec():
        return lend_copy(win.at[0, pl.ds(span, span)], hwin.at[pl.ds(span, span)], 0)

    def lent_prev(start, size):
        return lend_copy(prev.at[pl.ds(start, size)], hprev.at[pl.ds(start, size)], 1)

    def lent_halo(way):
        return pltpu.make_async_remote_copy(
            src_ref=hwin.at[pl.ds(span, span)],
            dst_ref=hwin.at[pl.ds(0 if way == 0 else 2 * span, span)],
            send_sem=eh_send.at[way], recv_sem=eh_recv.at[way],
            device_id=(up if way == 0 else down, z), device_id_type=MESH,
        )

    def help_copy(c):
        row = pl.multiple_of(span + c * bs + far * rows, rows)
        return pltpu.make_async_remote_copy(
            src_ref=hout.at[c], dst_ref=win.at[1, pl.ds(row, rows)],
            send_sem=r_send, recv_sem=r_recv,
            device_id=(orb, partner), device_id_type=MESH,
        )

    def all_help():
        whole = prev.at[pl.ds(0, rb * rows)]
        return pltpu.make_async_remote_copy(
            src_ref=whole, dst_ref=whole, send_sem=r_send, recv_sem=r_recv,
            device_id=(orb, partner), device_id_type=MESH,
        )

    def halo_copy(k, way, start, size):
        src = win.at[k, pl.ds(span + start, size)]
        dst = win.at[k, pl.ds((0 if way == 0 else 2 * span) + start, size)]
        return pltpu.make_async_remote_copy(
            src_ref=src, dst_ref=dst,
            send_sem=h_send.at[k, way], recv_sem=h_recv.at[k, way],
            device_id=(up if way == 0 else down, z), device_id_type=MESH,
        )

    loads[1].wait()
    for way in range(2):
        halo_copy(0, way, 0, span).start()
    loads[2].wait()

    @pl.when(is_end)
    def _():
        lent_vec().start()
        for i in range(rb):
            lent_prev(pl.multiple_of(i * bs + far * rows, rows), rows).start()

    def piece(k, i, start, size):
        total = jnp.dot(
            dense[i, pl.ds(start, size), :],
            win[k - 1, pl.ds(i * bs, depth), :],
            preferred_element_type=jnp.float32,
        )
        here = pl.multiple_of(i * bs + start, rows)
        there = pl.multiple_of(span + here, rows)
        if k == 1:
            before = prev[pl.ds(here, size), :]
        else:
            before = win[k - 2, pl.ds(there, size), :]
        win[k, pl.ds(there, size), :] = (
            2.0 * total - before.astype(jnp.float32)
        ).astype(win.dtype)
        for way in range(2):
            halo_copy(k, way, here, size).start()

    def help_piece(c, q):
        base = pl.multiple_of(q * rows, rows)
        total = jnp.dot(
            dense[c, pl.ds(base, rows), :],
            hwin[pl.ds(c * bs, depth), :],
            preferred_element_type=jnp.float32,
        )
        before = hprev[pl.ds(pl.multiple_of(c * bs + base, rows), rows), :]
        hout[c] = (2.0 * total - before.astype(jnp.float32)).astype(hout.dtype)
        help_copy(c).start()

    def unpack(c, q, side):
        lo, hi = chunks[c]
        for s in range(lo, hi):
            stage[s + side * (slots + 1)] = full[q, s]
        base = pl.multiple_of(q * rows, rows)
        for o in range(offs):
            dense[c, pl.ds(base, rows), o * bs:(o + 1) * bs] = stage[
                slot_of[c * offs + o] + side * (slots + 1)
            ]

    base_z = pl.multiple_of(z * rows, rows)
    for i in range(rb):
        for o in range(offs):
            mask = pattern_ref[i, o].astype(jnp.float32).astype(tl.dtype)
            dense[i, pl.ds(base_z, rows), o * bs:(o + 1) * bs] = tl[i * offs + o] * mask
    for way in range(2):
        halo_copy(0, way, 0, span).wait_recv()
    for i in range(rb):
        piece(1, i, base_z, rows)

    def hop(d, carry):
        @pl.when(jnp.logical_and(helps, d == n_probe - 2))
        def _():
            lent_vec().wait_recv()
            for way in range(2):
                lent_halo(way).start()

        for c in range(rb):
            for side in range(2):
                q = z - d if side == 0 else z + d
                valid = q >= 0 if side == 0 else q < n_probe

                @pl.when(valid)
                def _():
                    tile_copy(side, d, c, q).wait_recv()

                    @pl.when(has_next[side])
                    def _():
                        tile_copy(side, d + 1, c, q).start()

            for side in range(2):
                q = z - d if side == 0 else z + d
                valid = q >= 0 if side == 0 else q < n_probe

                @pl.when(valid)
                def _():
                    unpack(c, q, side)
                    piece(1, c, pl.multiple_of(q * rows, rows), rows)

            @pl.when(jnp.logical_and(helps, d == n_probe - 2))
            def _():
                if c == 0:
                    lent_prev(0, rb * rows).wait_recv()
                    for way in range(2):
                        lent_halo(way).wait_recv()
                help_piece(c, far)
        return carry

    stage[2 * slots + 1] = jnp.zeros((rows, bs), stage.dtype)
    lax.fori_loop(1, n_probe - 1, hop, 0)

    @pl.when(is_end)
    def _():
        all_help().wait_recv()
        base = pl.multiple_of(far * rows, rows)
        for i in range(rb):
            for way in range(2):
                halo_copy(1, way, pl.multiple_of(i * bs + base, rows), rows).start()
        for way in range(2):
            halo_copy(1, way, 0, span).wait_recv()
        near = pl.multiple_of(jnp.where(z == 0, 0, rows), rows)
        for i in range(rb):
            piece(2, i, near, bs - rows)
        for c in range(rb):
            lo, hi = chunks[c]
            part = full.at[far, pl.ds(lo, hi - lo)]
            pltpu.make_async_remote_copy(
                src_ref=part, dst_ref=part,
                send_sem=g_send.at[0, n_probe - 2],
                recv_sem=g_recv.at[jnp.where(z == 0, 1, 0), n_probe - 2, c],
                device_id=(orb, partner), device_id_type=MESH,
            ).wait_recv()
            unpack(c, far, 0)
            piece(2, c, base, rows)

    loads[3].wait()

    def moment(value, start):
        sign = (2 * signs[pl.ds(start, bs), :] - 1).astype(jnp.float32)
        return jnp.sum(sign * value.astype(jnp.float32), axis=0, keepdims=True)

    def dot(i, first, blocks, k):
        return jnp.dot(
            dense[i, :, (first - i) * bs:(first - i + blocks) * bs],
            win[k, pl.ds(first * bs, blocks * bs), :],
            preferred_element_type=jnp.float32,
        )

    def own_part(k):
        for i in range(rb):
            acc[i] = dot(i, rb, rb, k - 1)

    def value_of(k, i):
        image = acc[i] + dot(i, i, rb - i, k - 1) + dot(i, 2 * rb, i + 1, k - 1)
        before = win[k - 2, pl.ds(span + i * bs, bs), :].astype(jnp.float32)
        return (2.0 * image - before).astype(win.dtype)

    def rest_part(k):
        for way in range(2):
            halo_copy(k - 1, way, 0, span).wait_recv()
        for i in range(rb):
            win[k, pl.ds(span + i * bs, bs), :] = value_of(k, i)
            for way in range(2):
                halo_copy(k, way, i * bs, bs).start()

    def step_sum(k):
        total = jnp.zeros((1, pc), jnp.float32)
        for i in range(rb):
            total += moment(win[k, pl.ds(span + i * bs, bs), :], i * bs)
        return total

    @pl.when(jnp.logical_not(is_end))
    def _():
        own_part(2)
        rest_part(2)

    own_part(3)
    sums = [step_sum(1), step_sum(2)]
    rest_part(3)
    outs = [pltpu.make_async_copy(win.at[3, pl.ds(span, span)], older_hbm, out_sem.at[0])]
    outs[0].start()
    own_part(4)
    sums.append(step_sum(3))
    for way in range(2):
        halo_copy(3, way, 0, span).wait_recv()
    last_sum = jnp.zeros((1, pc), jnp.float32)
    for i in range(rb):
        value = value_of(4, i)
        last[pl.ds(i * bs, bs), :] = value
        last_sum += moment(value, i * bs)
    sums.append(last_sum)
    outs.append(pltpu.make_async_copy(last, newest_hbm, out_sem.at[1]))
    outs[1].start()
    mbuf[orb, 0:STEPS, :] = jnp.concatenate(sums, axis=0)

    def moment_copy(j):
        return pltpu.make_async_remote_copy(
            src_ref=mbuf.at[orb], dst_ref=mbuf.at[orb],
            send_sem=m_send, recv_sem=m_recv,
            device_id=(lax.rem(orb + j, n_orb), z), device_id_type=MESH,
        )

    def send_moment(j, carry):
        moment_copy(j).start()
        return carry

    lax.fori_loop(1, n_orb, send_moment, 0)

    for k in range(STEPS):
        for way in range(2):
            halo_copy(k, way, 0, span).wait_send()

    @pl.when(is_end)
    def _():
        lent_vec().wait_send()
        lent_prev(0, rb * rows).wait_send()

    @pl.when(helps)
    def _():
        for way in range(2):
            lent_halo(way).wait_send()
        all_help().wait_send()

    def sent(d, carry):
        for side in range(2):
            q = z + 1 - d if side == 0 else z - 1 + d
            valid = q >= 0 if side == 0 else q < n_probe

            @pl.when(jnp.logical_and(valid, has_next[side]))
            def _():
                pltpu.make_async_remote_copy(
                    src_ref=full.at[q], dst_ref=full.at[q],
                    send_sem=g_send.at[side, d - 1], recv_sem=g_recv.at[side, d - 1, 0],
                    device_id=(orb, z + 1 if side == 0 else z - 1), device_id_type=MESH,
                ).wait_send()
        return carry

    lax.fori_loop(1, n_probe, sent, 0)

    others = mbuf.at[pl.ds(0, n_orb - 1)]
    arrived = pltpu.make_async_remote_copy(
        src_ref=others, dst_ref=others, send_sem=m_send, recv_sem=m_recv,
        device_id=(up, z), device_id_type=MESH,
    )
    arrived.wait_recv()
    arrived.wait_send()
    result = mbuf[0]
    for j in range(1, n_orb):
        result = result + mbuf[j]
    moments_ref[...] = result[0:STEPS] * (1.0 / math.sqrt(n_orb * span))
    for out in outs:
        out.wait()


def body(tiles, pattern, signs, previous, current):
    n_orb, n_probe = lax.axis_size("orb"), lax.axis_size("probe")
    rb, offs, rows, bs = tiles.shape
    pc = previous.shape[1]
    slots = LIVE_PER_ROW * rb
    span = rb * bs
    bf16, f32 = jnp.bfloat16, jnp.float32
    anywhere = pl.BlockSpec(memory_space=pl.ANY)
    older, newest, moments = pl.pallas_call(
        functools.partial(kernel, n_orb, n_probe, rb, offs, rows, bs, pc),
        out_shape=(
            jax.ShapeDtypeStruct((span, pc), bf16),
            jax.ShapeDtypeStruct((span, pc), bf16),
            jax.ShapeDtypeStruct((STEPS, pc), f32),
        ),
        in_specs=[pl.BlockSpec(memory_space=pltpu.HBM)] * 5,
        out_specs=(anywhere, anywhere, pl.BlockSpec(memory_space=pltpu.VMEM)),
        scratch_shapes=[
            pltpu.VMEM((rb * offs, rows, bs), bf16),
            pltpu.VMEM((span, pc), jnp.int32),
            pltpu.VMEM((span, pc), bf16),
            pltpu.VMEM((n_probe, slots, rows, bs), bf16),
            pltpu.VMEM((2 * (slots + 1), rows, bs), bf16),
            pltpu.VMEM((rb, bs, offs * bs), bf16),
            pltpu.VMEM((STEPS, 3 * span, pc), bf16),
            pltpu.VMEM((span, pc), bf16),
            pltpu.VMEM((rb, bs, pc), f32),
            pltpu.VMEM((n_orb, 8, pc), f32),
            pltpu.VMEM((3 * span, pc), bf16),
            pltpu.VMEM((span, pc), bf16),
            pltpu.VMEM((rb, rows, pc), bf16),
            pltpu.SMEM((rb, offs), jnp.int32),
            pltpu.SMEM((rb * offs,), jnp.int32),
            pltpu.SMEM((rb * offs + 1,), jnp.int32),
            pltpu.SemaphoreType.DMA((5,)),
            pltpu.SemaphoreType.DMA((2,)),
            pltpu.SemaphoreType.DMA((2, n_probe - 1)),
            pltpu.SemaphoreType.DMA((2, n_probe - 1, rb)),
            pltpu.SemaphoreType.DMA((STEPS, 2)),
            pltpu.SemaphoreType.DMA((STEPS, 2)),
            pltpu.SemaphoreType.DMA,
            pltpu.SemaphoreType.DMA,
            pltpu.SemaphoreType.DMA((2,)),
            pltpu.SemaphoreType.DMA((2,)),
            pltpu.SemaphoreType.DMA((2,)),
            pltpu.SemaphoreType.DMA((2,)),
            pltpu.SemaphoreType.DMA,
            pltpu.SemaphoreType.DMA,
        ],
        compiler_params=pltpu.CompilerParams(
            collective_id=0, has_side_effects=True, vmem_limit_bytes=62 * 2**20
        ),
    )(pattern, tiles.reshape(rb * offs, rows, bs), signs, previous, current)
    return older, newest, moments


def solution(mesh):
    placed = (
        P("orb", None, "probe", None),
        P("orb", None),
        P("orb", "probe"),
        P("orb", "probe"),
        P("orb", "probe"),
    )
    return jax.shard_map(
        body,
        mesh=mesh,
        in_specs=placed,
        out_specs=(P("orb", "probe"), P("orb", "probe"), P(None, "probe")),
        check_vma=False,
    )
```

```python
import functools
import math

import jax
import jax.numpy as jnp
from jax import lax
from jax.experimental import pallas as pl
from jax.experimental.pallas import tpu as pltpu
from jax.sharding import PartitionSpec as P

STEPS = 4
LIVE_PER_ROW = 7
LEAST_PER_ROW = 4
MESH = pl.DeviceIdType.MESH


def chunk_bounds(row_blocks, offsets):
    slots = LIVE_PER_ROW * row_blocks
    return [
        min(offsets * (i + 1), slots - LEAST_PER_ROW * (row_blocks - 1 - i))
        for i in range(row_blocks)
    ]


def kernel(
    n_orb, n_probe, rb, offs, rows, bs, pc,
    pattern_hbm, tiles_hbm, signs_hbm, previous_hbm, current_hbm,
    older_hbm, newest_hbm, moments_ref,
    tl, signs, prev, full, stage, dense, win, last, acc, mbuf, hwin, hprev, hout, pattern_ref, slot_of, nxt,
    in_sem, out_sem, g_send, g_recv, h_send, h_recv, m_send, m_recv,
    e_send, e_recv, eh_send, eh_recv, r_send, r_recv,
):
    slots = LIVE_PER_ROW * rb
    span = rb * bs
    depth = offs * bs
    bounds = chunk_bounds(rb, offs)
    chunks = list(zip([0] + bounds[:-1], bounds))
    orb = lax.axis_index("orb")
    z = lax.axis_index("probe")
    up = lax.rem(orb + 1, n_orb)
    down = lax.rem(orb + n_orb - 1, n_orb)

    loads = [
        pltpu.make_async_copy(tiles_hbm, tl, in_sem.at[0]),
        pltpu.make_async_copy(current_hbm, win.at[0, pl.ds(span, span)], in_sem.at[1]),
        pltpu.make_async_copy(previous_hbm, prev, in_sem.at[2]),
        pltpu.make_async_copy(signs_hbm, signs, in_sem.at[3]),
        pltpu.make_async_copy(pattern_hbm, pattern_ref, in_sem.at[4]),
    ]
    for load in loads:
        load.start()

    barrier = pltpu.get_barrier_semaphore()

    def greet(j, carry):
        pl.semaphore_signal(
            barrier, inc=1, device_id=(lax.rem(orb + j, n_orb), z), device_id_type=MESH
        )
        return carry

    lax.fori_loop(1, n_orb, greet, 0)

    @pl.when(z > 0)
    def _():
        pl.semaphore_signal(barrier, inc=1, device_id=(orb, z - 1), device_id_type=MESH)

    @pl.when(z < n_probe - 1)
    def _():
        pl.semaphore_signal(barrier, inc=1, device_id=(orb, z + 1), device_id_type=MESH)

    loads[4].wait()
    count = jnp.int32(0)
    for j in range(rb * offs):
        live = pattern_ref[j // offs, j % offs] == 1
        slot_of[j] = jnp.where(live, count, slots)
        count = count + live.astype(jnp.int32)
    following = jnp.int32(rb * offs - 1)
    nxt[rb * offs] = following
    for j in reversed(range(rb * offs)):
        live = pattern_ref[j // offs, j % offs] == 1
        following = jnp.where(live, j, following)
        nxt[j] = following
    stage[slots] = jnp.zeros((rows, bs), stage.dtype)

    loads[0].wait()
    at = nxt[0]
    for s in range(slots):
        full[z, s] = tl[at]
        at = nxt[at + 1]

    ends = (z > 0).astype(jnp.int32) + (z < n_probe - 1).astype(jnp.int32)
    pl.semaphore_wait(barrier, n_orb - 1 + ends)

    def tile_copy(side, d, c, q):
        lo, hi = chunks[c]
        piece = full.at[q, pl.ds(lo, hi - lo)]
        to = z + 1 if side == 0 else z - 1
        return pltpu.make_async_remote_copy(
            src_ref=piece, dst_ref=piece,
            send_sem=g_send.at[side, d - 1, c], recv_sem=g_recv.at[side, d - 1, c],
            device_id=(orb, to), device_id_type=MESH,
        )

    has_next = (z < n_probe - 1, z > 0)
    for c in range(rb):
        for side in range(2):
            @pl.when(has_next[side])
            def _():
                tile_copy(side, 1, c, z).start()

    low = z < n_probe // 2
    is_end = jnp.logical_or(z == 0, z == n_probe - 1)
    helps = jnp.logical_or(z == 1, z == n_probe - 2)
    partner = jnp.where(
        is_end, jnp.where(low, 1, n_probe - 2), jnp.where(low, 0, n_probe - 1)
    )
    far = jnp.where(low, n_probe - 1, 0)

    def lend_copy(src, dst, which):
        return pltpu.make_async_remote_copy(
            src_ref=src, dst_ref=dst,
            send_sem=e_send.at[which], recv_sem=e_recv.at[which],
            device_id=(orb, partner), device_id_type=MESH,
        )

    def lent_vec():
        return lend_copy(win.at[0, pl.ds(span, span)], hwin.at[pl.ds(span, span)], 0)

    def lent_prev(start, size):
        return lend_copy(prev.at[pl.ds(start, size)], hprev.at[pl.ds(start, size)], 1)

    def lent_halo(way):
        return pltpu.make_async_remote_copy(
            src_ref=hwin.at[pl.ds(span, span)],
            dst_ref=hwin.at[pl.ds(0 if way == 0 else 2 * span, span)],
            send_sem=eh_send.at[way], recv_sem=eh_recv.at[way],
            device_id=(up if way == 0 else down, z), device_id_type=MESH,
        )

    def help_copy(c):
        row = pl.multiple_of(span + c * bs + far * rows, rows)
        return pltpu.make_async_remote_copy(
            src_ref=hout.at[c], dst_ref=win.at[1, pl.ds(row, rows)],
            send_sem=r_send, recv_sem=r_recv,
            device_id=(orb, partner), device_id_type=MESH,
        )

    def all_help():
        whole = prev.at[pl.ds(0, rb * rows)]
        return pltpu.make_async_remote_copy(
            src_ref=whole, dst_ref=whole, send_sem=r_send, recv_sem=r_recv,
            device_id=(orb, partner), device_id_type=MESH,
        )

    def halo_copy(k, way, start, size):
        src = win.at[k, pl.ds(span + start, size)]
        dst = win.at[k, pl.ds((0 if way == 0 else 2 * span) + start, size)]
        return pltpu.make_async_remote_copy(
            src_ref=src, dst_ref=dst,
            send_sem=h_send.at[k, way], recv_sem=h_recv.at[k, way],
            device_id=(up if way == 0 else down, z), device_id_type=MESH,
        )

    loads[1].wait()
    for way in range(2):
        halo_copy(0, way, 0, span).start()
    loads[2].wait()

    @pl.when(is_end)
    def _():
        lent_vec().start()
        for i in range(rb):
            lent_prev(pl.multiple_of(i * bs + far * rows, rows), rows).start()

    def piece(k, i, start, size):
        total = jnp.dot(
            dense[i, pl.ds(start, size), :],
            win[k - 1, pl.ds(i * bs, depth), :],
            preferred_element_type=jnp.float32,
        )
        here = pl.multiple_of(i * bs + start, rows)
        there = pl.multiple_of(span + here, rows)
        if k == 1:
            before = prev[pl.ds(here, size), :]
        else:
            before = win[k - 2, pl.ds(there, size), :]
        win[k, pl.ds(there, size), :] = (
            2.0 * total - before.astype(jnp.float32)
        ).astype(win.dtype)
        for way in range(2):
            halo_copy(k, way, here, size).start()

    def help_piece(c, q):
        base = pl.multiple_of(q * rows, rows)
        total = jnp.dot(
            dense[c, pl.ds(base, rows), :],
            hwin[pl.ds(c * bs, depth), :],
            preferred_element_type=jnp.float32,
        )
        before = hprev[pl.ds(pl.multiple_of(c * bs + base, rows), rows), :]
        hout[c] = (2.0 * total - before.astype(jnp.float32)).astype(hout.dtype)
        help_copy(c).start()

    def unpack(c, q, side):
        lo, hi = chunks[c]
        for s in range(lo, hi):
            stage[s + side * (slots + 1)] = full[q, s]
        base = pl.multiple_of(q * rows, rows)
        for o in range(offs):
            dense[c, pl.ds(base, rows), o * bs:(o + 1) * bs] = stage[
                slot_of[c * offs + o] + side * (slots + 1)
            ]

    base_z = pl.multiple_of(z * rows, rows)
    for i in range(rb):
        for o in range(offs):
            mask = pattern_ref[i, o].astype(jnp.float32).astype(tl.dtype)
            dense[i, pl.ds(base_z, rows), o * bs:(o + 1) * bs] = tl[i * offs + o] * mask
    for way in range(2):
        halo_copy(0, way, 0, span).wait_recv()
    for i in range(rb):
        piece(1, i, base_z, rows)

    def hop(d, carry):
        @pl.when(jnp.logical_and(helps, d == n_probe - 2))
        def _():
            lent_vec().wait_recv()
            for way in range(2):
                lent_halo(way).start()

        for c in range(rb):
            for side in range(2):
                q = z - d if side == 0 else z + d
                valid = q >= 0 if side == 0 else q < n_probe

                @pl.when(valid)
                def _():
                    tile_copy(side, d, c, q).wait_recv()

                    @pl.when(has_next[side])
                    def _():
                        tile_copy(side, d, c, q).wait_send()
                        tile_copy(side, d + 1, c, q).start()

            for side in range(2):
                q = z - d if side == 0 else z + d
                valid = q >= 0 if side == 0 else q < n_probe

                @pl.when(valid)
                def _():
                    unpack(c, q, side)
                    piece(1, c, pl.multiple_of(q * rows, rows), rows)

            @pl.when(jnp.logical_and(helps, d == n_probe - 2))
            def _():
                if c == 0:
                    lent_prev(0, rb * rows).wait_recv()
                    for way in range(2):
                        lent_halo(way).wait_recv()
                help_piece(c, far)
        return carry

    stage[2 * slots + 1] = jnp.zeros((rows, bs), stage.dtype)
    lax.fori_loop(1, n_probe - 1, hop, 0)

    @pl.when(is_end)
    def _():
        all_help().wait_recv()
        base = pl.multiple_of(far * rows, rows)
        for i in range(rb):
            for way in range(2):
                halo_copy(1, way, pl.multiple_of(i * bs + base, rows), rows).start()
        for way in range(2):
            halo_copy(1, way, 0, span).wait_recv()
        near = pl.multiple_of(jnp.where(z == 0, 0, rows), rows)
        for i in range(rb):
            piece(2, i, near, bs - rows)
        for c in range(rb):
            lo, hi = chunks[c]
            part = full.at[far, pl.ds(lo, hi - lo)]
            pltpu.make_async_remote_copy(
                src_ref=part, dst_ref=part,
                send_sem=g_send.at[0, n_probe - 2, c],
                recv_sem=g_recv.at[jnp.where(z == 0, 1, 0), n_probe - 2, c],
                device_id=(orb, partner), device_id_type=MESH,
            ).wait_recv()
            unpack(c, far, 0)
            piece(2, c, base, rows)

    loads[3].wait()

    def moment(value, start):
        sign = (2 * signs[pl.ds(start, bs), :] - 1).astype(jnp.float32)
        return jnp.sum(sign * value.astype(jnp.float32), axis=0, keepdims=True)

    def dot(i, first, blocks, k):
        return jnp.dot(
            dense[i, :, (first - i) * bs:(first - i + blocks) * bs],
            win[k, pl.ds(first * bs, blocks * bs), :],
            preferred_element_type=jnp.float32,
        )

    def own_part(k):
        for i in range(rb):
            acc[i] = dot(i, rb, rb, k - 1)

    def value_of(k, i):
        image = acc[i] + dot(i, i, rb - i, k - 1) + dot(i, 2 * rb, i + 1, k - 1)
        before = win[k - 2, pl.ds(span + i * bs, bs), :].astype(jnp.float32)
        return (2.0 * image - before).astype(win.dtype)

    def rest_part(k):
        for way in range(2):
            halo_copy(k - 1, way, 0, span).wait_recv()
        for i in range(rb):
            win[k, pl.ds(span + i * bs, bs), :] = value_of(k, i)
            for way in range(2):
                halo_copy(k, way, i * bs, bs).start()

    def step_sum(k):
        total = jnp.zeros((1, pc), jnp.float32)
        for i in range(rb):
            total += moment(win[k, pl.ds(span + i * bs, bs), :], i * bs)
        return total

    @pl.when(jnp.logical_not(is_end))
    def _():
        own_part(2)
        rest_part(2)

    own_part(3)
    sums = [step_sum(1), step_sum(2)]
    rest_part(3)
    outs = [pltpu.make_async_copy(win.at[3, pl.ds(span, span)], older_hbm, out_sem.at[0])]
    outs[0].start()
    own_part(4)
    sums.append(step_sum(3))
    for way in range(2):
        halo_copy(3, way, 0, span).wait_recv()
    last_sum = jnp.zeros((1, pc), jnp.float32)
    for i in range(rb):
        value = value_of(4, i)
        last[pl.ds(i * bs, bs), :] = value
        last_sum += moment(value, i * bs)
    sums.append(last_sum)
    outs.append(pltpu.make_async_copy(last, newest_hbm, out_sem.at[1]))
    outs[1].start()
    mbuf[orb, 0:STEPS, :] = jnp.concatenate(sums, axis=0)

    def moment_copy(j):
        return pltpu.make_async_remote_copy(
            src_ref=mbuf.at[orb], dst_ref=mbuf.at[orb],
            send_sem=m_send, recv_sem=m_recv,
            device_id=(lax.rem(orb + j, n_orb), z), device_id_type=MESH,
        )

    def send_moment(j, carry):
        moment_copy(j).start()
        return carry

    lax.fori_loop(1, n_orb, send_moment, 0)

    for k in range(STEPS):
        for way in range(2):
            halo_copy(k, way, 0, span).wait_send()

    @pl.when(is_end)
    def _():
        lent_vec().wait_send()
        lent_prev(0, rb * rows).wait_send()

    @pl.when(helps)
    def _():
        for way in range(2):
            lent_halo(way).wait_send()
        all_help().wait_send()

    for side in range(2):
        @pl.when(has_next[side])
        def _():
            final = z + 1 if side == 0 else n_probe - z
            for c in range(rb):
                tile_copy(side, final, c, z).wait_send()

    others = mbuf.at[pl.ds(0, n_orb - 1)]
    arrived = pltpu.make_async_remote_copy(
        src_ref=others, dst_ref=others, send_sem=m_send, recv_sem=m_recv,
        device_id=(up, z), device_id_type=MESH,
    )
    arrived.wait_recv()
    arrived.wait_send()
    result = mbuf[0]
    for j in range(1, n_orb):
        result = result + mbuf[j]
    moments_ref[...] = result[0:STEPS] * (1.0 / math.sqrt(n_orb * span))
    for out in outs:
        out.wait()


def body(tiles, pattern, signs, previous, current):
    n_orb, n_probe = lax.axis_size("orb"), lax.axis_size("probe")
    rb, offs, rows, bs = tiles.shape
    pc = previous.shape[1]
    slots = LIVE_PER_ROW * rb
    span = rb * bs
    bf16, f32 = jnp.bfloat16, jnp.float32
    anywhere = pl.BlockSpec(memory_space=pl.ANY)
    older, newest, moments = pl.pallas_call(
        functools.partial(kernel, n_orb, n_probe, rb, offs, rows, bs, pc),
        out_shape=(
            jax.ShapeDtypeStruct((span, pc), bf16),
            jax.ShapeDtypeStruct((span, pc), bf16),
            jax.ShapeDtypeStruct((STEPS, pc), f32),
        ),
        in_specs=[pl.BlockSpec(memory_space=pltpu.HBM)] * 5,
        out_specs=(anywhere, anywhere, pl.BlockSpec(memory_space=pltpu.VMEM)),
        scratch_shapes=[
            pltpu.VMEM((rb * offs, rows, bs), bf16),
            pltpu.VMEM((span, pc), jnp.int32),
            pltpu.VMEM((span, pc), bf16),
            pltpu.VMEM((n_probe, slots, rows, bs), bf16),
            pltpu.VMEM((2 * (slots + 1), rows, bs), bf16),
            pltpu.VMEM((rb, bs, offs * bs), bf16),
            pltpu.VMEM((STEPS, 3 * span, pc), bf16),
            pltpu.VMEM((span, pc), bf16),
            pltpu.VMEM((rb, bs, pc), f32),
            pltpu.VMEM((n_orb, 8, pc), f32),
            pltpu.VMEM((3 * span, pc), bf16),
            pltpu.VMEM((span, pc), bf16),
            pltpu.VMEM((rb, rows, pc), bf16),
            pltpu.SMEM((rb, offs), jnp.int32),
            pltpu.SMEM((rb * offs,), jnp.int32),
            pltpu.SMEM((rb * offs + 1,), jnp.int32),
            pltpu.SemaphoreType.DMA((5,)),
            pltpu.SemaphoreType.DMA((2,)),
            pltpu.SemaphoreType.DMA((2, n_probe - 1, rb)),
            pltpu.SemaphoreType.DMA((2, n_probe - 1, rb)),
            pltpu.SemaphoreType.DMA((STEPS, 2)),
            pltpu.SemaphoreType.DMA((STEPS, 2)),
            pltpu.SemaphoreType.DMA,
            pltpu.SemaphoreType.DMA,
            pltpu.SemaphoreType.DMA((2,)),
            pltpu.SemaphoreType.DMA((2,)),
            pltpu.SemaphoreType.DMA((2,)),
            pltpu.SemaphoreType.DMA((2,)),
            pltpu.SemaphoreType.DMA,
            pltpu.SemaphoreType.DMA,
        ],
        compiler_params=pltpu.CompilerParams(
            collective_id=0, has_side_effects=True, vmem_limit_bytes=62 * 2**20
        ),
    )(pattern, tiles.reshape(rb * offs, rows, bs), signs, previous, current)
    return older, newest, moments


def solution(mesh):
    placed = (
        P("orb", None, "probe", None),
        P("orb", None),
        P("orb", "probe"),
        P("orb", "probe"),
        P("orb", "probe"),
    )
    return jax.shard_map(
        body,
        mesh=mesh,
        in_specs=placed,
        out_specs=(P("orb", "probe"), P("orb", "probe"), P(None, "probe")),
        check_vma=False,
    )
```
